32 devices in a mesh: aux: 16 (over z, y, core), occ: 2 (over x).
Axes of the slice: x: 2, y: 2, z: 4, core: 2. Of those that a mesh axis runs over, the one named last changes fastest.
Arguments:
- integrals: bfloat16 [128, 21, 512, 512], P('aux', None, 'occ'), may hold values from -0.40234375 to 0.40234375
- orbitals: bfloat16 [3072, 384], replicated, may hold values from -0.109375 to 0.109375
Outputs:
- k_tiles: float32 [512, 21, 512], P('aux', None, 'occ')
The draws below stay inside these ranges and needn't reach their ends.
All inputs are finite; a program needn't handle non-finite values.
Results may differ from the reference program's by a relative error of at most 0.0017.
Values may be sent and summed in bfloat16 or wider, within the bound.
A program may use at most 192 MiB of HBM per device.

```python
import jax
import jax.numpy as jnp
from jax import lax

TILE = 512
NB = 6
OCC = 384
NAUX = 128
N = 3072
NT = 21


def block_scale(own_key, dims, shards, smallest, top_value):
    def one(axis_at, parts):
        steps = jax.random.uniform(jax.random.fold_in(jax.random.fold_in(own_key, 6), axis_at), (parts,), jnp.float32, smallest / len(shards), top_value / len(shards))
        return jnp.repeat(jnp.exp(steps), dims[axis_at] // parts).reshape((-1,) + (1,) * (len(dims) - axis_at - 1))

    level = one(*shards[0])
    for cut in shards[1:]:
        level = level * one(*cut)
    return level


def bell_draw(own_key, extent, width, reach, cuts=(), held_as=jnp.bfloat16):
    array = width * jax.random.normal(own_key, extent, jnp.float32)
    if cuts:
        array = array * block_scale(own_key, extent, cuts, -0.22, 0.18)
    return jnp.clip(array, -reach, reach).astype(held_as)


def setup_inputs(seed: int = 0) -> dict:
    key_list = jax.random.split(jax.random.key(seed), 3)
    return {
        "integrals": bell_draw(key_list[0], (NAUX, NT, TILE, TILE), ((NAUX * OCC) ** -0.25), 0.40234375, ((0, 16), (2, 2))),
        "orbitals": bell_draw(key_list[1], (N, OCC), N ** -0.5, 0.109375),
    }


def tile_index(row_index, col_index):
    return row_index * NB - row_index * (row_index - 1) // 2 + col_index - row_index


def reference(integrals, orbitals):
    coeffs = orbitals.astype(jnp.float32)

    def per_slab(slab_tiles):
        band_list = []
        for row_index in range(NB):
            pieces = []
            for col_index in range(NB):
                if col_index >= row_index:
                    pieces.append(slab_tiles[tile_index(row_index, col_index)])
                else:
                    pieces.append(slab_tiles[tile_index(col_index, row_index)].T)
            band_list.append(jnp.concatenate(pieces, axis=1))
        full_matrix = jnp.concatenate(band_list, axis=0).astype(jnp.float32)
        return jnp.dot(full_matrix, coeffs, precision=lax.Precision.HIGHEST).astype(jnp.bfloat16)

    half_transform = lax.map(per_slab, integrals)
    flat_half = jnp.transpose(half_transform, (1, 0, 2)).reshape(NB * TILE, -1).astype(jnp.float32)
    exchange = jnp.dot(flat_half, flat_half.T, precision=lax.Precision.HIGHEST)
    out_tiles = []
    for row_index in range(NB):
        for col_index in range(row_index, NB):
            out_tiles.append(exchange[row_index * TILE:(row_index + 1) * TILE, col_index * TILE:(col_index + 1) * TILE])
    return jnp.stack(out_tiles, axis=1)
```

```python
import functools

import jax
import jax.numpy as jnp
from jax import lax
from jax.experimental import pallas as pl
from jax.experimental.pallas import tpu as pltpu
from jax.sharding import PartitionSpec as P

NB = 6


def first_tile(row_index, block_count):
    return row_index * block_count - row_index * (row_index - 1) // 2


def column_body(integrals, orbitals):
    occ_parts = lax.axis_size("occ")
    my_index = lax.axis_index("occ")
    slab_count = integrals.shape[0]
    row_width = integrals.shape[2]
    tile_size = integrals.shape[3]
    occ_count = orbitals.shape[1]
    block_count = NB
    own_terms = []
    for row_index in range(block_count):
        tile_begin = first_tile(row_index, block_count)
        tile_span = block_count - row_index
        coeffs = orbitals[row_index * tile_size :].reshape(tile_span, tile_size, occ_count)
        own_terms.append(
            jnp.einsum(
                "pkrm,kmi->pri",
                integrals[:, tile_begin : tile_begin + tile_span],
                coeffs,
                preferred_element_type=jnp.float32,
            )
        )
    own_coeffs = lax.dynamic_index_in_dim(
        orbitals.reshape(block_count, occ_parts, row_width, occ_count), my_index, 1, keepdims=False
    )
    partial_list = []
    for col_index in range(1, block_count):
        stacked = jnp.stack(
            [
                integrals[:, first_tile(row_index, block_count) + col_index - row_index]
                for row_index in range(col_index)
            ],
            axis=1,
        )
        partial_list.append(
            jnp.einsum(
                "pkrc,kri->pci", stacked, own_coeffs[:col_index], preferred_element_type=jnp.float32
            )
        )
    partials = jnp.stack(partial_list, axis=1).reshape(
        slab_count, block_count - 1, occ_parts, row_width, occ_count
    )
    received = lax.all_to_all(
        partials.astype(jnp.bfloat16), "occ", split_axis=2, concat_axis=2, tiled=True
    ).astype(partials.dtype)
    summed = jnp.sum(received, axis=2)
    lower_terms = [summed[:, position] for position in range(block_count - 1)]
    totals = [own_terms[0]] + [
        own_terms[row_index] + lower_terms[row_index - 1] for row_index in range(1, block_count)
    ]
    half_transform = (
        jnp.stack(totals, axis=1)
        .reshape(slab_count, block_count * row_width, occ_count)
        .astype(jnp.bfloat16)
    )
    gathered = lax.all_gather(half_transform, "occ", axis=1, tiled=True)
    gathered_view = gathered.reshape(slab_count, occ_parts, block_count, row_width, occ_count)
    row_blocks = [
        gathered_view[:, :, row_index].reshape(slab_count, tile_size, occ_count)
        for row_index in range(block_count)
    ]
    column_terms = []
    for row_index in range(block_count):
        picked = row_blocks[row_index]
        column_terms.append(
            jnp.einsum(
                "pri,pci->rc",
                picked,
                half_transform[:, row_index * row_width :],
                preferred_element_type=jnp.float32,
            )
        )
    return lax.psum_scatter(
        jnp.concatenate(column_terms, axis=1).reshape(
            tile_size // lax.axis_size("aux") * lax.axis_size("aux"), -1, row_width
        ),
        "aux",
        scatter_dimension=0,
        tiled=True,
    )

VMEM_LIMIT = 40 * 1024 * 1024


def tile_at(row_index, col_index):
    low, high = min(row_index, col_index), max(row_index, col_index)
    return first_tile(low, NB) + high - low


def half_kernel(block, owned, where, coeffs, *refs):
    tiles, refs = refs[:NB], refs[NB:]
    row_width, tile_size = tiles[0].shape[2:]
    me = where[0]
    mine = pl.ds(pl.multiple_of(me * row_width, row_width), row_width)
    own = sum(
        lax.dot_general(
            coeffs[:, at * tile_size : (at + 1) * tile_size],
            tiles[at][0, 0],
            (((1,), (1,)), ((), ())),
            preferred_element_type=jnp.float32,
        )
        for at in range(block, NB)
    )
    lower = None
    for at in range(block):
        rows = pl.ds(pl.multiple_of(at * tile_size + me * row_width, row_width), row_width)
        term = jnp.dot(coeffs[:, rows], tiles[at][0, 0], preferred_element_type=jnp.float32)
        lower = term if lower is None else lower + term
    if not owned:
        out, total = refs
        if block == 0:
            out[0] = own.astype(out.dtype)
            return
        total[...] = lower
        total[:, mine] += own
        out[0] = total[...].astype(out.dtype)
        return
    received, out, total = refs
    if block == 0:
        other = pl.ds(pl.multiple_of((1 - me) * row_width, row_width), row_width)
        total[:, mine] = own
        total[:, other] = received[0].astype(jnp.float32)
    else:
        total[...] = lower + received[0].astype(jnp.float32)
        total[:, mine] += own
    out[...] = total[...].T.astype(out.dtype)


def half_call(block, owned, where, coeffs, integrals, received=None):
    slab_count, _, row_width, tile_size = integrals.shape
    occ_count = coeffs.shape[0]
    count = slab_count // 2
    width = row_width if block == 0 else tile_size
    at = 1 if owned else 2

    def tile_spec(tile):
        return pl.BlockSpec(
            (1, 1, row_width, tile_size), lambda p, where: (where[at] + p, tile, 0, 0)
        )

    moved = pl.BlockSpec((1, occ_count, width), lambda p, where: (p, 0, 0))
    in_specs = [pl.BlockSpec(coeffs.shape, lambda p, where: (0, 0))]
    in_specs += [tile_spec(tile_at(block, other)) for other in range(NB)]
    args = [coeffs] + [integrals] * NB
    if owned:
        in_specs.append(moved)
        args.append(received)
        out_shape = jax.ShapeDtypeStruct((tile_size, count * occ_count), jnp.bfloat16)
        out_spec = pl.BlockSpec((tile_size, occ_count), lambda p, where: (0, p))
    else:
        out_shape = jax.ShapeDtypeStruct((count, occ_count, width), jnp.bfloat16)
        out_spec = moved
    return pl.pallas_call(
        functools.partial(half_kernel, block, owned),
        out_shape=out_shape,
        grid_spec=pltpu.PrefetchScalarGridSpec(
            num_scalar_prefetch=1,
            grid=(count,),
            in_specs=in_specs,
            out_specs=out_spec,
            scratch_shapes=[pltpu.VMEM((occ_count, tile_size), jnp.float32)],
        ),
        compiler_params=pltpu.CompilerParams(vmem_limit_bytes=VMEM_LIMIT),
        cost_estimate=pl.CostEstimate(
            flops=2 * count * NB * row_width * tile_size * occ_count,
            bytes_accessed=count * NB * row_width * tile_size * 2 + coeffs.size * 2,
            transcendentals=0,
        ),
        name=f"half_{'own' if owned else 'send'}_{block}",
    )(where, *args)


def bit_reverse(value, bits):
    return sum(((value >> bit) & 1) << (bits - 1 - bit) for bit in range(bits))


def tile_kernel(bits, where, *refs):
    halves, (keep, send, total) = refs[:-3], refs[-3:]
    parts = 2**bits
    rows, cols = keep.shape[3:]
    for at, left in enumerate(halves):
        total[...] = lax.dot_general(
            left[...],
            halves[-1][...],
            (((1,), (1,)), ((), ())),
            preferred_element_type=jnp.float32,
        )
        for place in range(parts):
            out = keep if place < parts // 2 else send
            owner = lax.bitwise_xor(where[3], jnp.int32(bit_reverse(place, bits)))
            picked = pl.ds(pl.multiple_of(owner * rows, rows), rows)
            for side in range(2):
                half = lax.bitwise_xor(where[0], jnp.int32(side))
                out[place % (parts // 2), side, at] = total[
                    picked, pl.ds(pl.multiple_of(half * cols, cols), cols)
                ]


def tile_call(bits, where, halves):
    parts = 2**bits
    tile_size, depth = halves[0].shape
    count = len(halves)
    out = jax.ShapeDtypeStruct(
        (parts // 2, 2, count, tile_size // parts, tile_size // 2), jnp.float32
    )
    return pl.pallas_call(
        functools.partial(tile_kernel, bits),
        out_shape=[out, out],
        in_specs=[pl.BlockSpec(memory_space=pltpu.SMEM)]
        + [pl.BlockSpec(memory_space=pltpu.VMEM)] * count,
        out_specs=[pl.BlockSpec(memory_space=pltpu.VMEM)] * 2,
        scratch_shapes=[pltpu.VMEM((tile_size, tile_size), jnp.float32)],
        compiler_params=pltpu.CompilerParams(vmem_limit_bytes=VMEM_LIMIT),
        cost_estimate=pl.CostEstimate(
            flops=2 * count * tile_size * tile_size * depth,
            bytes_accessed=count * (tile_size * depth * 2 + tile_size * tile_size * 4),
            transcendentals=0,
        ),
        name=f"tiles_{count - 1}",
    )(where, *halves)


def slab_body(integrals, orbitals):
    parts = lax.axis_size("aux")
    bits = parts.bit_length() - 1
    me = lax.axis_index("occ")
    count = integrals.shape[0] // 2
    where = jnp.stack(
        [me, me * count, (1 - me) * count, lax.axis_index("aux")]
    ).astype(jnp.int32)
    coeffs = orbitals.T
    swap = [(0, 1), (1, 0)]
    received = []
    for block in range(NB):
        sent = half_call(block, False, where, coeffs, integrals)
        if block >= 2:
            sent, received[-2] = lax.optimization_barrier((sent, received[-2]))
        received.append(lax.ppermute(sent, "occ", swap))
    halves, columns = [], []
    for block in range(NB):
        halves.append(half_call(block, True, where, coeffs, integrals, received[block]))
        keep, send = tile_call(bits, where, halves)
        for step in range(bits):
            pairs = [(at, at ^ (1 << step)) for at in range(parts)]
            came = lax.ppermute(send, "aux", pairs)
            if step < bits - 1:
                middle = keep.shape[0] // 2
                send = keep[middle:] + came[middle:]
                keep = keep[:middle] + came[:middle]
            else:
                send = keep[:, 1] + came[:, 1]
                keep = keep[:, 0] + came[:, 0]
        columns.append((keep + lax.ppermute(send, "occ", swap))[0])
    order = [columns[high][low] for low in range(NB) for high in range(low, NB)]
    return jnp.stack(order, axis=1)


def body(integrals, orbitals):
    parts = lax.axis_size("aux")
    slab_count, _, row_width, tile_size = integrals.shape
    fits = (
        lax.axis_size("occ") == 2
        and slab_count % 2 == 0
        and parts >= 2
        and parts & (parts - 1) == 0
        and tile_size % (8 * parts) == 0
        and row_width % 128 == 0
        and orbitals.shape[1] % 128 == 0
    )
    return (slab_body if fits else column_body)(integrals, orbitals)


def solution(mesh):
    placed = (P("aux", None, "occ", None), P())
    return jax.shard_map(
        body, mesh=mesh, in_specs=placed, out_specs=P("aux", None, "occ"), check_vma=False
    )
```

```python
import functools

import jax
import jax.numpy as jnp
from jax import lax
from jax.experimental import pallas as pl
from jax.experimental.pallas import tpu as pltpu
from jax.sharding import PartitionSpec as P

NB = 6


def first_tile(row_index, block_count):
    return row_index * block_count - row_index * (row_index - 1) // 2


def column_body(integrals, orbitals):
    occ_parts = lax.axis_size("occ")
    my_index = lax.axis_index("occ")
    slab_count = integrals.shape[0]
    row_width = integrals.shape[2]
    tile_size = integrals.shape[3]
    occ_count = orbitals.shape[1]
    block_count = NB
    own_terms = []
    for row_index in range(block_count):
        tile_begin = first_tile(row_index, block_count)
        tile_span = block_count - row_index
        coeffs = orbitals[row_index * tile_size :].reshape(tile_span, tile_size, occ_count)
        own_terms.append(
            jnp.einsum(
                "pkrm,kmi->pri",
                integrals[:, tile_begin : tile_begin + tile_span],
                coeffs,
                preferred_element_type=jnp.float32,
            )
        )
    own_coeffs = lax.dynamic_index_in_dim(
        orbitals.reshape(block_count, occ_parts, row_width, occ_count), my_index, 1, keepdims=False
    )
    partial_list = []
    for col_index in range(1, block_count):
        stacked = jnp.stack(
            [
                integrals[:, first_tile(row_index, block_count) + col_index - row_index]
                for row_index in range(col_index)
            ],
            axis=1,
        )
        partial_list.append(
            jnp.einsum(
                "pkrc,kri->pci", stacked, own_coeffs[:col_index], preferred_element_type=jnp.float32
            )
        )
    partials = jnp.stack(partial_list, axis=1).reshape(
        slab_count, block_count - 1, occ_parts, row_width, occ_count
    )
    received = lax.all_to_all(
        partials.astype(jnp.bfloat16), "occ", split_axis=2, concat_axis=2, tiled=True
    ).astype(partials.dtype)
    summed = jnp.sum(received, axis=2)
    lower_terms = [summed[:, position] for position in range(block_count - 1)]
    totals = [own_terms[0]] + [
        own_terms[row_index] + lower_terms[row_index - 1] for row_index in range(1, block_count)
    ]
    half_transform = (
        jnp.stack(totals, axis=1)
        .reshape(slab_count, block_count * row_width, occ_count)
        .astype(jnp.bfloat16)
    )
    gathered = lax.all_gather(half_transform, "occ", axis=1, tiled=True)
    gathered_view = gathered.reshape(slab_count, occ_parts, block_count, row_width, occ_count)
    row_blocks = [
        gathered_view[:, :, row_index].reshape(slab_count, tile_size, occ_count)
        for row_index in range(block_count)
    ]
    column_terms = []
    for row_index in range(block_count):
        picked = row_blocks[row_index]
        column_terms.append(
            jnp.einsum(
                "pri,pci->rc",
                picked,
                half_transform[:, row_index * row_width :],
                preferred_element_type=jnp.float32,
            )
        )
    return lax.psum_scatter(
        jnp.concatenate(column_terms, axis=1).reshape(
            tile_size // lax.axis_size("aux") * lax.axis_size("aux"), -1, row_width
        ),
        "aux",
        scatter_dimension=0,
        tiled=True,
    )

VMEM_LIMIT = 40 * 1024 * 1024


def took(microseconds):
    return pl.CostEstimate(
        flops=int(microseconds * 1.15e9), bytes_accessed=1, transcendentals=0
    )


DEPTH = 2
OWN, SEND, TILE_COST = 20, 1, 0.1


def tile_at(row_index, col_index):
    low, high = min(row_index, col_index), max(row_index, col_index)
    return first_tile(low, NB) + high - low


def half_kernel(block, owned, where, coeffs, *refs):
    tiles, refs = refs[:NB], refs[NB:]
    row_width, tile_size = tiles[0].shape[2:]
    me = where[0]
    mine = pl.ds(pl.multiple_of(me * row_width, row_width), row_width)
    own = sum(
        lax.dot_general(
            coeffs[:, at * tile_size : (at + 1) * tile_size],
            tiles[at][0, 0],
            (((1,), (1,)), ((), ())),
            preferred_element_type=jnp.float32,
        )
        for at in range(block, NB)
    )
    lower = None
    for at in range(block):
        rows = pl.ds(pl.multiple_of(at * tile_size + me * row_width, row_width), row_width)
        term = jnp.dot(coeffs[:, rows], tiles[at][0, 0], preferred_element_type=jnp.float32)
        lower = term if lower is None else lower + term
    if not owned:
        out, total = refs
        if block == 0:
            out[0] = own.astype(out.dtype)
            return
        total[...] = lower
        total[:, mine] += own
        out[0] = total[...].astype(out.dtype)
        return
    received, out, total = refs
    if block == 0:
        other = pl.ds(pl.multiple_of((1 - me) * row_width, row_width), row_width)
        total[:, mine] = own
        total[:, other] = received[0].astype(jnp.float32)
    else:
        total[...] = lower + received[0].astype(jnp.float32)
        total[:, mine] += own
    out[...] = total[...].T.astype(out.dtype)


def half_call(block, owned, where, coeffs, integrals, received=None):
    slab_count, _, row_width, tile_size = integrals.shape
    occ_count = coeffs.shape[0]
    count = slab_count // 2
    width = row_width if block == 0 else tile_size
    at = 1 if owned else 2

    def tile_spec(tile):
        return pl.BlockSpec(
            (1, 1, row_width, tile_size), lambda p, where: (where[at] + p, tile, 0, 0)
        )

    moved = pl.BlockSpec((1, occ_count, width), lambda p, where: (p, 0, 0))
    in_specs = [pl.BlockSpec(coeffs.shape, lambda p, where: (0, 0))]
    in_specs += [tile_spec(tile_at(block, other)) for other in range(NB)]
    args = [coeffs] + [integrals] * NB
    if owned:
        in_specs.append(moved)
        args.append(received)
        out_shape = jax.ShapeDtypeStruct((tile_size, count * occ_count), jnp.bfloat16)
        out_spec = pl.BlockSpec((tile_size, occ_count), lambda p, where: (0, p))
    else:
        out_shape = jax.ShapeDtypeStruct((count, occ_count, width), jnp.bfloat16)
        out_spec = moved
    return pl.pallas_call(
        functools.partial(half_kernel, block, owned),
        out_shape=out_shape,
        grid_spec=pltpu.PrefetchScalarGridSpec(
            num_scalar_prefetch=1,
            grid=(count,),
            in_specs=in_specs,
            out_specs=out_spec,
            scratch_shapes=[pltpu.VMEM((occ_count, tile_size), jnp.float32)],
        ),
        compiler_params=pltpu.CompilerParams(vmem_limit_bytes=VMEM_LIMIT),
        cost_estimate=took(OWN if owned else SEND),
        name=f"half_{'own' if owned else 'send'}_{block}",
    )(where, *args)


def tile_groups(block, bits):
    plain = tuple(range(bits))
    if block < NB - 1 or bits < 3:
        return [(tuple(range(block + 1)), plain)]
    turned = (0,) + tuple(range(2, bits)) + (1,)
    middle = (block + 1) // 2
    return [(tuple(range(middle)), plain), (tuple(range(middle, block + 1)), turned)]


def relative_owner(place, order):
    bits = len(order)
    return sum(((place >> (bits - 1 - step)) & 1) << order[step] for step in range(bits))


def tile_kernel(groups, where, *refs):
    count = sum(len(members) for members, _ in groups)
    halves, outs, total = refs[:count], refs[count:-1], refs[-1]
    for group, (members, order) in enumerate(groups):
        keep, send = outs[2 * group : 2 * group + 2]
        parts = 2 ** len(order)
        rows, cols = keep.shape[3:]
        for at, tile in enumerate(members):
            total[...] = lax.dot_general(
                halves[tile][...],
                halves[-1][...],
                (((1,), (1,)), ((), ())),
                preferred_element_type=jnp.float32,
            )
            for place in range(parts):
                out = keep if place < parts // 2 else send
                owner = lax.bitwise_xor(where[3], jnp.int32(relative_owner(place, order)))
                picked = pl.ds(pl.multiple_of(owner * rows, rows), rows)
                for side in range(2):
                    half = lax.bitwise_xor(where[0], jnp.int32(side))
                    out[place % (parts // 2), side, at] = total[
                        picked, pl.ds(pl.multiple_of(half * cols, cols), cols)
                    ]


def tile_call(groups, where, halves):
    tile_size, depth = halves[0].shape
    count = len(halves)
    parts = 2 ** len(groups[0][1])
    outs = []
    for members, _ in groups:
        outs += [
            jax.ShapeDtypeStruct(
                (parts // 2, 2, len(members), tile_size // parts, tile_size // 2), jnp.float32
            )
        ] * 2
    return pl.pallas_call(
        functools.partial(tile_kernel, groups),
        out_shape=outs,
        in_specs=[pl.BlockSpec(memory_space=pltpu.SMEM)]
        + [pl.BlockSpec(memory_space=pltpu.VMEM)] * count,
        out_specs=[pl.BlockSpec(memory_space=pltpu.VMEM)] * len(outs),
        scratch_shapes=[pltpu.VMEM((tile_size, tile_size), jnp.float32)],
        compiler_params=pltpu.CompilerParams(vmem_limit_bytes=VMEM_LIMIT),
        cost_estimate=took(TILE_COST * count),
        name=f"tiles_{count - 1}",
    )(where, *halves)


class Reduction:
    def __init__(self, members, order, keep, send):
        self.members, self.order = members, order
        self.keep, self.send = keep, send
        self.step = 0

    def advance(self):
        if self.step < len(self.order):
            bit = 1 << self.order[self.step]
            came = lax.ppermute(
                self.send, "aux", [(at, at ^ bit) for at in range(2 ** len(self.order))]
            )
            self.step += 1
            if self.step < len(self.order):
                middle = self.keep.shape[0] // 2
                self.send = self.keep[middle:] + came[middle:]
                self.keep = self.keep[:middle] + came[:middle]
            else:
                self.send = self.keep[:, 1] + came[:, 1]
                self.keep = self.keep[:, 0] + came[:, 0]
        elif self.step == len(self.order):
            self.step += 1
            self.keep = self.keep + lax.ppermute(self.send, "occ", [(0, 1), (1, 0)])
            self.send = None


def hold(value, reductions):
    live = [one for one in reductions if one.send is not None]
    value, sends = lax.optimization_barrier((value, [one.send for one in live]))
    for one, send in zip(live, sends):
        one.send = send
    return value


def slab_body(integrals, orbitals):
    bits = lax.axis_size("aux").bit_length() - 1
    me = lax.axis_index("occ")
    count = integrals.shape[0] // 2
    where = jnp.stack(
        [me, me * count, (1 - me) * count, lax.axis_index("aux")]
    ).astype(jnp.int32)
    coeffs = orbitals.T
    swap = [(0, 1), (1, 0)]
    received = []
    for block in range(NB):
        sent = half_call(block, False, where, coeffs, integrals)
        if block >= DEPTH:
            sent, received[-DEPTH] = lax.optimization_barrier((sent, received[-DEPTH]))
        received.append(lax.ppermute(sent, "occ", swap))
    halves, running = [], []
    for block in range(NB):
        for one in running:
            one.advance()
        half = half_call(block, True, where, coeffs, integrals, received[block])
        halves.append(hold(half, running))
        groups = tile_groups(block, bits)
        parts = tile_call(groups, where, halves)
        fresh = [
            Reduction(members, order, *parts[2 * at : 2 * at + 2])
            for at, (members, order) in enumerate(groups)
        ]
        if block < NB - 1:
            running += fresh
    for one in fresh:
        one.advance()
    for step in range(bits):
        for one in running:
            if one.step < bits:
                one.advance()
        fresh_sends, sends = lax.optimization_barrier(
            ([one.send for one in fresh], [one.send for one in running if one.send is not None])
        )
        for one, send in zip(fresh, fresh_sends):
            one.send = send
        for one, send in zip([one for one in running if one.send is not None], sends):
            one.send = send
        for one in running + fresh:
            if one.step < bits and one in fresh:
                one.advance()
    columns = {}
    for one in running + fresh:
        while one.send is not None:
            one.advance()
    at = 0
    every = running + fresh
    for block in range(NB):
        seen = 0
        while seen <= block:
            for place, tile in enumerate(every[at].members):
                columns[tile, block] = every[at].keep[0, place]
                seen += 1
            at += 1
    return jnp.stack(
        [columns[low, high] for low in range(NB) for high in range(low, NB)], axis=1
    )


def body(integrals, orbitals):
    parts = lax.axis_size("aux")
    slab_count, _, row_width, tile_size = integrals.shape
    fits = (
        lax.axis_size("occ") == 2
        and slab_count % 2 == 0
        and parts >= 2
        and parts & (parts - 1) == 0
        and tile_size % (8 * parts) == 0
        and row_width % 128 == 0
        and orbitals.shape[1] % 128 == 0
    )
    return (slab_body if fits else column_body)(integrals, orbitals)


def solution(mesh):
    placed = (P("aux", None, "occ", None), P())
    return jax.shard_map(
        body, mesh=mesh, in_specs=placed, out_specs=P("aux", None, "occ"), check_vma=False
    )
```

```python
import functools

import jax
import jax.numpy as jnp
from jax import lax
from jax.experimental import pallas as pl
from jax.experimental.pallas import tpu as pltpu
from jax.sharding import PartitionSpec as P

NB = 6


def first_tile(row_index, block_count):
    return row_index * block_count - row_index * (row_index - 1) // 2


def column_body(integrals, orbitals):
    occ_parts = lax.axis_size("occ")
    my_index = lax.axis_index("occ")
    slab_count = integrals.shape[0]
    row_width = integrals.shape[2]
    tile_size = integrals.shape[3]
    occ_count = orbitals.shape[1]
    block_count = NB
    own_terms = []
    for row_index in range(block_count):
        tile_begin = first_tile(row_index, block_count)
        tile_span = block_count - row_index
        coeffs = orbitals[row_index * tile_size :].reshape(tile_span, tile_size, occ_count)
        own_terms.append(
            jnp.einsum(
                "pkrm,kmi->pri",
                integrals[:, tile_begin : tile_begin + tile_span],
                coeffs,
                preferred_element_type=jnp.float32,
            )
        )
    own_coeffs = lax.dynamic_index_in_dim(
        orbitals.reshape(block_count, occ_parts, row_width, occ_count), my_index, 1, keepdims=False
    )
    partial_list = []
    for col_index in range(1, block_count):
        stacked = jnp.stack(
            [
                integrals[:, first_tile(row_index, block_count) + col_index - row_index]
                for row_index in range(col_index)
            ],
            axis=1,
        )
        partial_list.append(
            jnp.einsum(
                "pkrc,kri->pci", stacked, own_coeffs[:col_index], preferred_element_type=jnp.float32
            )
        )
    partials = jnp.stack(partial_list, axis=1).reshape(
        slab_count, block_count - 1, occ_parts, row_width, occ_count
    )
    received = lax.all_to_all(
        partials.astype(jnp.bfloat16), "occ", split_axis=2, concat_axis=2, tiled=True
    ).astype(partials.dtype)
    summed = jnp.sum(received, axis=2)
    lower_terms = [summed[:, position] for position in range(block_count - 1)]
    totals = [own_terms[0]] + [
        own_terms[row_index] + lower_terms[row_index - 1] for row_index in range(1, block_count)
    ]
    half_transform = (
        jnp.stack(totals, axis=1)
        .reshape(slab_count, block_count * row_width, occ_count)
        .astype(jnp.bfloat16)
    )
    gathered = lax.all_gather(half_transform, "occ", axis=1, tiled=True)
    gathered_view = gathered.reshape(slab_count, occ_parts, block_count, row_width, occ_count)
    row_blocks = [
        gathered_view[:, :, row_index].reshape(slab_count, tile_size, occ_count)
        for row_index in range(block_count)
    ]
    column_terms = []
    for row_index in range(block_count):
        picked = row_blocks[row_index]
        column_terms.append(
            jnp.einsum(
                "pri,pci->rc",
                picked,
                half_transform[:, row_index * row_width :],
                preferred_element_type=jnp.float32,
            )
        )
    return lax.psum_scatter(
        jnp.concatenate(column_terms, axis=1).reshape(
            tile_size // lax.axis_size("aux") * lax.axis_size("aux"), -1, row_width
        ),
        "aux",
        scatter_dimension=0,
        tiled=True,
    )

VMEM_LIMIT = 40 * 1024 * 1024


def took(microseconds):
    return pl.CostEstimate(
        flops=int(microseconds * 1.15e9), bytes_accessed=1, transcendentals=0
    )


DEPTH = 2
OWN, SEND, TILE_COST = 20, 1, 0.1


def tile_at(row_index, col_index):
    low, high = min(row_index, col_index), max(row_index, col_index)
    return first_tile(low, NB) + high - low


def half_kernel(block, owned, where, coeffs, *refs):
    tiles, refs = refs[:NB], refs[NB:]
    row_width, tile_size = tiles[0].shape[2:]
    me = where[0]
    mine = pl.ds(pl.multiple_of(me * row_width, row_width), row_width)
    own = sum(
        lax.dot_general(
            coeffs[:, at * tile_size : (at + 1) * tile_size],
            tiles[at][0, 0],
            (((1,), (1,)), ((), ())),
            preferred_element_type=jnp.float32,
        )
        for at in range(block, NB)
    )
    lower = None
    for at in range(block):
        rows = pl.ds(pl.multiple_of(at * tile_size + me * row_width, row_width), row_width)
        term = jnp.dot(coeffs[:, rows], tiles[at][0, 0], preferred_element_type=jnp.float32)
        lower = term if lower is None else lower + term
    if not owned:
        out, total = refs
        if block == 0:
            out[0] = own.astype(out.dtype)
            return
        total[...] = lower
        total[:, mine] += own
        out[0] = total[...].astype(out.dtype)
        return
    received, out, total = refs
    if block == 0:
        other = pl.ds(pl.multiple_of((1 - me) * row_width, row_width), row_width)
        total[:, mine] = own
        total[:, other] = received[0].astype(jnp.float32)
    else:
        total[...] = lower + received[0].astype(jnp.float32)
        total[:, mine] += own
    out[...] = total[...].T.astype(out.dtype)


def half_call(block, owned, where, coeffs, integrals, received=None):
    slab_count, _, row_width, tile_size = integrals.shape
    occ_count = coeffs.shape[0]
    count = slab_count // 2
    width = row_width if block == 0 else tile_size
    at = 1 if owned else 2

    def tile_spec(tile):
        return pl.BlockSpec(
            (1, 1, row_width, tile_size), lambda p, where: (where[at] + p, tile, 0, 0)
        )

    moved = pl.BlockSpec((1, occ_count, width), lambda p, where: (p, 0, 0))
    in_specs = [pl.BlockSpec(coeffs.shape, lambda p, where: (0, 0))]
    in_specs += [tile_spec(tile_at(block, other)) for other in range(NB)]
    args = [coeffs] + [integrals] * NB
    if owned:
        in_specs.append(moved)
        args.append(received)
        out_shape = jax.ShapeDtypeStruct((tile_size, count * occ_count), jnp.bfloat16)
        out_spec = pl.BlockSpec((tile_size, occ_count), lambda p, where: (0, p))
    else:
        out_shape = jax.ShapeDtypeStruct((count, occ_count, width), jnp.bfloat16)
        out_spec = moved
    return pl.pallas_call(
        functools.partial(half_kernel, block, owned),
        out_shape=out_shape,
        grid_spec=pltpu.PrefetchScalarGridSpec(
            num_scalar_prefetch=1,
            grid=(count,),
            in_specs=in_specs,
            out_specs=out_spec,
            scratch_shapes=[pltpu.VMEM((occ_count, tile_size), jnp.float32)],
        ),
        compiler_params=pltpu.CompilerParams(vmem_limit_bytes=VMEM_LIMIT),
        cost_estimate=took(OWN if owned else SEND),
        name=f"half_{'own' if owned else 'send'}_{block}",
    )(where, *args)


def tile_groups(block, bits):
    plain = tuple(range(bits))
    if block < NB - 1 or bits < 3:
        return [(tuple(range(block + 1)), plain)]
    middle = (block + 1) // 2
    return [(tuple(range(middle)), plain), (tuple(range(middle, block + 1)), plain)]


def relative_owner(place, order):
    bits = len(order)
    return sum(((place >> (bits - 1 - step)) & 1) << order[step] for step in range(bits))


def tile_kernel(groups, where, *refs):
    count = sum(len(members) for members, _ in groups)
    halves, outs, total = refs[:count], refs[count:-1], refs[-1]
    for group, (members, order) in enumerate(groups):
        keep, send = outs[2 * group : 2 * group + 2]
        parts = 2 ** len(order)
        rows, cols = keep.shape[3:]
        for at, tile in enumerate(members):
            total[...] = lax.dot_general(
                halves[tile][...],
                halves[-1][...],
                (((1,), (1,)), ((), ())),
                preferred_element_type=jnp.float32,
            )
            for place in range(parts):
                out = keep if place < parts // 2 else send
                owner = lax.bitwise_xor(where[3], jnp.int32(relative_owner(place, order)))
                picked = pl.ds(pl.multiple_of(owner * rows, rows), rows)
                for side in range(2):
                    half = lax.bitwise_xor(where[0], jnp.int32(side))
                    out[place % (parts // 2), side, at] = total[
                        picked, pl.ds(pl.multiple_of(half * cols, cols), cols)
                    ]


def tile_call(groups, where, halves):
    tile_size, depth = halves[0].shape
    count = len(halves)
    parts = 2 ** len(groups[0][1])
    outs = []
    for members, _ in groups:
        outs += [
            jax.ShapeDtypeStruct(
                (parts // 2, 2, len(members), tile_size // parts, tile_size // 2), jnp.float32
            )
        ] * 2
    return pl.pallas_call(
        functools.partial(tile_kernel, groups),
        out_shape=outs,
        in_specs=[pl.BlockSpec(memory_space=pltpu.SMEM)]
        + [pl.BlockSpec(memory_space=pltpu.VMEM)] * count,
        out_specs=[pl.BlockSpec(memory_space=pltpu.VMEM)] * len(outs),
        scratch_shapes=[pltpu.VMEM((tile_size, tile_size), jnp.float32)],
        compiler_params=pltpu.CompilerParams(vmem_limit_bytes=VMEM_LIMIT),
        cost_estimate=took(TILE_COST * count),
        name=f"tiles_{count - 1}",
    )(where, *halves)


class Reduction:
    def __init__(self, members, order, keep, send):
        self.members, self.order = members, order
        self.keep, self.send = keep, send
        self.step = 0

    def advance(self):
        if self.step < len(self.order):
            bit = 1 << self.order[self.step]
            came = lax.ppermute(
                self.send, "aux", [(at, at ^ bit) for at in range(2 ** len(self.order))]
            )
            self.step += 1
            if self.step < len(self.order):
                middle = self.keep.shape[0] // 2
                self.send = self.keep[middle:] + came[middle:]
                self.keep = self.keep[:middle] + came[:middle]
            else:
                self.send = self.keep[:, 1] + came[:, 1]
                self.keep = self.keep[:, 0] + came[:, 0]
        elif self.step == len(self.order):
            self.step += 1
            self.keep = self.keep + lax.ppermute(self.send, "occ", [(0, 1), (1, 0)])
            self.send = None


def hold(value, reductions):
    live = [one for one in reductions if one.send is not None]
    value, sends = lax.optimization_barrier((value, [one.send for one in live]))
    for one, send in zip(live, sends):
        one.send = send
    return value


def slab_body(integrals, orbitals):
    bits = lax.axis_size("aux").bit_length() - 1
    me = lax.axis_index("occ")
    count = integrals.shape[0] // 2
    where = jnp.stack(
        [me, me * count, (1 - me) * count, lax.axis_index("aux")]
    ).astype(jnp.int32)
    coeffs = orbitals.T
    swap = [(0, 1), (1, 0)]
    received = []
    for block in range(NB):
        sent = half_call(block, False, where, coeffs, integrals)
        if block >= DEPTH:
            sent, received[-DEPTH] = lax.optimization_barrier((sent, received[-DEPTH]))
        received.append(lax.ppermute(sent, "occ", swap))
    halves, running = [], []
    for block in range(NB):
        for one in running:
            one.advance()
        half = half_call(block, True, where, coeffs, integrals, received[block])
        halves.append(hold(half, running))
        groups = tile_groups(block, bits)
        parts = tile_call(groups, where, halves)
        fresh = [
            Reduction(members, order, *parts[2 * at : 2 * at + 2])
            for at, (members, order) in enumerate(groups)
        ]
        if block < NB - 1:
            running += fresh
    for one in fresh:
        one.advance()
    for _ in range(bits):
        for one in running:
            if one.send is not None:
                one.advance()
        fresh_sends, held = lax.optimization_barrier(
            (
                [one.send for one in fresh],
                [one.keep if one.send is None else one.send for one in running],
            )
        )
        for one, send in zip(fresh, fresh_sends):
            one.send = send
            if one.step < bits:
                one.advance()
        for one, value in zip(running, held):
            if one.send is None:
                one.keep = value
            else:
                one.send = value
    columns = {}
    for one in running + fresh:
        while one.send is not None:
            one.advance()
    at = 0
    every = running + fresh
    for block in range(NB):
        seen = 0
        while seen <= block:
            for place, tile in enumerate(every[at].members):
                columns[tile, block] = every[at].keep[0, place]
                seen += 1
            at += 1
    return jnp.stack(
        [columns[low, high] for low in range(NB) for high in range(low, NB)], axis=1
    )


def body(integrals, orbitals):
    parts = lax.axis_size("aux")
    slab_count, _, row_width, tile_size = integrals.shape
    fits = (
        lax.axis_size("occ") == 2
        and slab_count % 2 == 0
        and parts >= 2
        and parts & (parts - 1) == 0
        and tile_size % (8 * parts) == 0
        and row_width % 128 == 0
        and orbitals.shape[1] % 128 == 0
    )
    return (slab_body if fits else column_body)(integrals, orbitals)


def solution(mesh):
    placed = (P("aux", None, "occ", None), P())
    return jax.shard_map(
        body, mesh=mesh, in_specs=placed, out_specs=P("aux", None, "occ"), check_vma=False
    )
```
